32 devices in a mesh: inner: 8 (over y, x, core), outer: 4 (over z).
Axes of the slice: x: 2, y: 2, z: 4, core: 2. Of those that a mesh axis runs over, the one named last changes fastest.
Arguments:
- samples: bfloat16 [16384, 4096], P(('inner', 'outer')), may hold values from -6 to 6
- sketch_matrix: bfloat16 [4096, 128], P('inner'), may hold values from -0.09375 to 0.09375
Outputs:
- basis: float32 [16384, 128], P(('inner', 'outer'))
- projection: float32 [4096, 128], P('inner')
- row_error: float32 [16384], P(('inner', 'outer'))
The draws below stay inside these ranges and needn't reach their ends.
All inputs are finite; a program needn't handle non-finite values.
Results may differ from the reference program's by a relative error of at most 0.0014.
Values may be sent and summed in bfloat16 or wider, within the bound.
No kernel may reach another device: no remote copies, remote signals or barrier semaphores. Data moves between devices by JAX's collectives and lax.ppermute only.
A program may use at most 64 MiB of HBM per device.

```python
import math
import jax
import jax.numpy as jnp
from jax import lax

D = 4096
K = 128
ROWS_DEV = 512
ROWS = 16384


def raised(values, own_key, source, target, blocks, factor):
    def block_of(dim):
        return (jnp.arange(values.shape[dim]) // (values.shape[dim] // blocks)).reshape((-1,) + (1,) * (values.ndim - 1 - dim))

    one_side = jax.random.permutation(own_key, blocks)[block_of(target)]
    other_side = (block_of(target) + blocks // 2) % blocks
    return jnp.where((block_of(source) == one_side) | (block_of(source) == other_side), factor * values, values)


def steps_of(own_key, dims, cuts, smallest, top_value):
    def one(axis_at, parts):
        heights = jax.random.uniform(jax.random.fold_in(jax.random.fold_in(own_key, 6), axis_at), (parts,), jnp.float32, smallest / len(cuts), top_value / len(cuts))
        return jnp.repeat(jnp.exp(heights), dims[axis_at] // parts).reshape((-1,) + (1,) * (len(dims) - axis_at - 1))

    factor_of = one(*cuts[0])
    for cut in cuts[1:]:
        factor_of = factor_of * one(*cut)
    return factor_of


def normal_values(rng, extent, deviation, reach, split=(), kind=jnp.bfloat16):
    array = deviation * jax.random.normal(rng, extent, jnp.float32)
    if split:
        array = array * steps_of(rng, extent, split, -0.22, 0.18)
    return jnp.clip(array, -reach, reach).astype(kind)


def heavy_noise(key, dims, width, reach, cuts, heavy, dtype=jnp.bfloat16):
    array = width * jax.random.normal(key, dims, jnp.float32)
    if cuts:
        array = array * steps_of(key, dims, cuts, -0.22, 0.18)
    return jnp.clip(raised(array, jax.random.fold_in(key, 3), *heavy), -reach, reach).astype(dtype)


def setup_inputs(seed: int = 0) -> dict:
    key_list = jax.random.split(jax.random.key(seed), 3)
    return {
        "samples": heavy_noise(key_list[0], (ROWS, D), 1.0, 6.0, ((0, 32),), (0, 1, 32, 2.75)),
        "sketch_matrix": normal_values(key_list[1], (D, K), D ** -0.5, 0.09375, ((0, 8),)),
    }


def reference(samples, sketch_matrix):
    sketch = jnp.dot(samples.astype(jnp.float32), sketch_matrix.astype(jnp.float32), preferred_element_type=jnp.float32)
    gram_matrix = jnp.dot(sketch.T, sketch, precision=lax.Precision.HIGHEST)
    lower_factor = jnp.linalg.cholesky(gram_matrix)
    basis = lax.linalg.triangular_solve(lower_factor, sketch, left_side=False, lower=True, transpose_a=True)
    basis = basis * math.sqrt(ROWS)
    basis_low = basis.astype(jnp.bfloat16)
    summed = lax.dot_general(samples.astype(jnp.float32), basis_low.astype(jnp.float32), (((0,), (0,)), ((), ())), preferred_element_type=jnp.float32)
    projection = summed * (math.sqrt(D) / ROWS)
    projection_low = projection.astype(jnp.bfloat16)

    def block_error(pair):
        rows_block, basis_block = pair
        recon = jnp.dot(basis_block.astype(jnp.float32), projection_low.T.astype(jnp.float32), preferred_element_type=jnp.float32) / math.sqrt(D)
        diff = rows_block.astype(jnp.float32) - recon
        return lax.optimization_barrier(jnp.sum(diff * diff, axis=1)) / D
    blocks = ROWS // ROWS_DEV
    errors = lax.map(block_error, (samples.reshape(blocks, ROWS_DEV, D), basis_low.reshape(blocks, ROWS_DEV, K)))
    return (basis, projection, errors.reshape(ROWS))
```

```python
import math

import jax
import jax.numpy as jnp
from jax import lax
from jax.sharding import PartitionSpec as P


def flipped(block, axis, mask):
    count = lax.axis_size(axis)
    return lax.ppermute(block, axis, [(low, low ^ mask) for low in range(count)])


def exact_dot(a, b, contract):
    return lax.dot_general(
        a, b, (contract, ((), ())), precision=lax.Precision.HIGHEST, preferred_element_type=jnp.float32
    )


def summed_over(value, axis):
    for level in range(lax.axis_size(axis).bit_length() - 1):
        value = value + flipped(value, axis, 1 << level)
    return value


def local(samples, sketch_matrix):
    inner = lax.axis_size("inner")
    outer = lax.axis_size("outer")
    rows, width = samples.shape
    rank = sketch_matrix.shape[1]
    total_rows = rows * inner * outer
    me = lax.axis_index("inner")
    mine = lax.axis_index("outer")
    piece = width // inner
    part = piece // outer
    evens = range(2, inner, 2)

    got = {0: sketch_matrix}
    for mask in reversed(evens):
        got[mask] = flipped(sketch_matrix, "inner", mask)
    even = jnp.concatenate([got[mask] for mask in range(0, inner, 2)])
    odd = flipped(even, "inner", 1)

    def columns(masks):
        return jnp.concatenate(
            [lax.dynamic_slice_in_dim(samples, (me ^ mask) * piece, piece, 1) for mask in masks], axis=1
        )

    even_columns = columns(range(0, inner, 2))
    odd_columns = columns(range(1, inner, 2))
    sketch = jnp.dot(even_columns, even, preferred_element_type=jnp.float32)
    sketch = sketch + jnp.dot(odd_columns, odd, preferred_element_type=jnp.float32)

    gram = exact_dot(sketch, sketch, ((0,), (0,)))
    high = sketch.astype(jnp.bfloat16)
    low = (sketch - high.astype(jnp.float32)).astype(jnp.bfloat16)
    both = jnp.concatenate([high, low], axis=1)

    def products(side):
        twice = lax.dot_general(side, both, (((0,), (0,)), ((), ())), preferred_element_type=jnp.float32)
        return twice[:, :rank] + twice[:, rank:]

    pieces = products(even_columns) + flipped(products(odd_columns), "inner", 1)
    pieces = pieces.reshape(inner // 2, piece, rank)
    own = pieces[0]
    for mask in reversed(evens):
        own = own + flipped(pieces[mask // 2], "inner", mask)
    share = lax.dynamic_slice_in_dim(own, mine * part, part, 0)
    for mask in range(1, outer):
        share = share + flipped(
            lax.dynamic_slice_in_dim(own, (mine ^ mask) * part, part, 0), "outer", mask
        )

    gram = summed_over(summed_over(gram, "inner"), "outer")
    lower_factor = jnp.linalg.cholesky(gram)
    inverse = lax.linalg.triangular_solve(
        lower_factor, jnp.eye(rank, dtype=jnp.float32), left_side=False, lower=True, transpose_a=True
    )

    basis = exact_dot(sketch, inverse * math.sqrt(total_rows), ((1,), (0,)))
    basis_low = basis.astype(jnp.bfloat16)

    share = exact_dot(share, inverse * (math.sqrt(width) / math.sqrt(total_rows)), ((1,), (0,)))
    projection = jnp.zeros((piece, rank), jnp.float32)
    projection = lax.dynamic_update_slice_in_dim(projection, share, mine * part, 0)
    for mask in range(1, outer):
        projection = lax.dynamic_update_slice_in_dim(
            projection, flipped(share, "outer", mask), (mine ^ mask) * part, 0
        )
    projection_low = projection.astype(jnp.bfloat16)

    got = {0: projection_low}
    for mask in reversed(evens):
        got[mask] = flipped(projection_low, "inner", mask)
    even = jnp.concatenate([got[mask] for mask in range(0, inner, 2)])
    odd = flipped(even, "inner", 1)

    def errors(side, factor):
        recon = lax.dot_general(
            basis_low, factor, (((1,), (1,)), ((), ())), preferred_element_type=jnp.float32
        ) * (1.0 / math.sqrt(width))
        diff = side.astype(jnp.float32) - recon
        return jnp.sum(diff * diff, axis=1)

    row_error = (errors(even_columns, even) + errors(odd_columns, odd)) / width
    return (basis, projection, row_error)


def solution(mesh):
    placed = (P(("inner", "outer"), None), P("inner", None))
    return jax.shard_map(
        local,
        mesh=mesh,
        in_specs=placed,
        out_specs=(P(("inner", "outer"), None), P("inner", None), P(("inner", "outer"))),
        check_vma=False,
    )
```

```python
import functools
import math

import jax
import jax.numpy as jnp
from jax import lax
from jax.experimental import pallas as pl
from jax.experimental.pallas import tpu as pltpu
from jax.sharding import PartitionSpec as P


def flipped(block, axis, mask):
    count = lax.axis_size(axis)
    return lax.ppermute(block, axis, [(low, low ^ mask) for low in range(count)])


def exact_dot(a, b, contract):
    return lax.dot_general(
        a, b, (contract, ((), ())), precision=lax.Precision.HIGHEST, preferred_element_type=jnp.float32
    )


def terms(value):
    high = value.astype(jnp.bfloat16).astype(jnp.float32)
    rest = value - high
    middle = rest.astype(jnp.bfloat16).astype(jnp.float32)
    return high, middle, rest - middle


def factor_kernel(block, gram_ref, out_ref, work, lines):
    n = gram_ref.shape[0]
    work[:, :n] = gram_ref[...]
    down = lax.broadcasted_iota(jnp.int32, (n, n), 0)
    across = lax.broadcasted_iota(jnp.int32, (n, n), 1)
    work[:, n:] = jnp.where(down == across, 1.0, 0.0)
    for top in range(0, n, block):
        line = [work[top + i : top + i + 1, :] for i in range(block)]
        corner = {}
        for i in range(block):
            for j in range(i + 1):
                corner[i, j] = jnp.broadcast_to(line[i][:, top + j : top + j + 1], (1, n))
        for j in range(block):
            scale = lax.rsqrt(corner[j, j])
            line[j] = line[j] * jnp.concatenate([scale, scale], axis=1)
            lines[j : j + 1, :] = line[j]
            for i in range(j + 1, block):
                corner[i, j] = corner[i, j] * scale
            for i in range(j + 1, block):
                for m in range(j + 1, i + 1):
                    corner[i, m] = corner[i, m] - corner[i, j] * corner[m, j]
                line[i] = line[i] - jnp.concatenate([corner[i, j]] * 2, axis=1) * line[j]
        done = lines[...]
        out_ref[top : top + block, :] = done[:, n:]
        if top + block < n:
            high, middle, small = terms(done)
            left = jnp.concatenate([high, high, middle, high, small, middle])[:, :n].astype(jnp.bfloat16)
            right = jnp.concatenate([high, middle, high, small, high, middle]).astype(jnp.bfloat16)
            work[...] -= lax.dot_general(
                left, right, (((0,), (0,)), ((), ())), preferred_element_type=jnp.float32
            )


def inverse_factor(gram, block=16):
    n = gram.shape[0]
    return pl.pallas_call(
        functools.partial(factor_kernel, block),
        out_shape=jax.ShapeDtypeStruct((n, n), jnp.float32),
        scratch_shapes=[pltpu.VMEM((n, 2 * n), jnp.float32), pltpu.VMEM((block, 2 * n), jnp.float32)],
        cost_estimate=pl.CostEstimate(flops=6_000_000_000, bytes_accessed=131072, transcendentals=128),
        name="inverse_factor",
    )(gram)


def local(samples, sketch_matrix):
    inner = lax.axis_size("inner")
    outer = lax.axis_size("outer")
    rows, width = samples.shape
    rank = sketch_matrix.shape[1]
    total_rows = rows * inner * outer
    me = lax.axis_index("inner")
    mine = lax.axis_index("outer")
    piece = width // inner
    part = piece // outer
    evens = range(2, inner, 2)

    got = {0: sketch_matrix}
    for mask in reversed(evens):
        got[mask] = flipped(sketch_matrix, "inner", mask)
    even = jnp.concatenate([got[mask] for mask in range(0, inner, 2)])

    def columns(masks):
        return jnp.concatenate(
            [lax.dynamic_slice_in_dim(samples, (me ^ mask) * piece, piece, 1) for mask in masks], axis=1
        )

    even_columns = columns(range(0, inner, 2))
    odd_columns = columns(range(1, inner, 2))
    even, even_columns, odd_columns = lax.optimization_barrier((even, even_columns, odd_columns))
    odd = flipped(even, "inner", 1)
    sketch = jnp.dot(even_columns, even, preferred_element_type=jnp.float32)
    sketch = sketch + jnp.dot(odd_columns, odd, preferred_element_type=jnp.float32)

    gram = exact_dot(sketch, sketch, ((0,), (0,)))
    rounded = lax.reduce_precision(sketch, 8, 7)
    high = rounded.astype(jnp.bfloat16)
    low = (sketch - rounded).astype(jnp.bfloat16)
    both = jnp.concatenate([high, low], axis=1)

    def products(side):
        twice = lax.dot_general(side, both, (((0,), (0,)), ((), ())), preferred_element_type=jnp.float32)
        return twice[:, :rank] + twice[:, rank:]

    pieces = products(even_columns) + flipped(products(odd_columns), "inner", 1)
    gram = gram + flipped(gram, "inner", 1)
    pieces = pieces.reshape(inner // 2, piece, rank)
    gram = gram + flipped(gram, "inner", 2)
    gram, near = lax.optimization_barrier((gram, pieces[1]))
    for level in range(2, inner.bit_length() - 1):
        gram = gram + flipped(gram, "inner", 1 << level)
    gram, *rest = lax.optimization_barrier((gram, *[pieces[mask // 2] for mask in reversed(evens[1:])]))
    own = pieces[0] + flipped(near, "inner", 2)
    for mask, block in zip(reversed(evens[1:]), rest):
        own = own + flipped(block, "inner", mask)
    for level in range(outer.bit_length() - 1):
        gram = gram + flipped(gram, "outer", 1 << level)
    gram, _ = lax.optimization_barrier((gram, own))
    share = lax.dynamic_slice_in_dim(own, mine * part, part, 0)
    for mask in range(1, outer):
        share = share + flipped(
            lax.dynamic_slice_in_dim(own, (mine ^ mask) * part, part, 0), "outer", mask
        )

    inverse = inverse_factor(gram)
    basis = exact_dot(sketch, inverse * math.sqrt(total_rows), ((1,), (1,)))
    basis_low = basis.astype(jnp.bfloat16)

    share = exact_dot(share, inverse * (math.sqrt(width) / math.sqrt(total_rows)), ((1,), (1,)))
    projection = jnp.zeros((piece, rank), jnp.float32)
    projection = lax.dynamic_update_slice_in_dim(projection, share, mine * part, 0)
    for mask in range(1, outer):
        projection = lax.dynamic_update_slice_in_dim(
            projection, flipped(share, "outer", mask), (mine ^ mask) * part, 0
        )
    projection_low = projection.astype(jnp.bfloat16)

    got = {0: projection_low}
    for mask in reversed(evens):
        got[mask] = flipped(projection_low, "inner", mask)
    even = jnp.concatenate([got[mask] for mask in range(0, inner, 2)])
    odd = flipped(even, "inner", 1)

    def errors(side, factor):
        recon = lax.dot_general(
            basis_low, factor, (((1,), (1,)), ((), ())), preferred_element_type=jnp.float32
        ) * (1.0 / math.sqrt(width))
        diff = side.astype(jnp.float32) - recon
        return jnp.sum(diff * diff, axis=1)

    row_error = (errors(even_columns, even) + errors(odd_columns, odd)) / width
    return (basis, projection, row_error)


def solution(mesh):
    placed = (P(("inner", "outer"), None), P("inner", None))
    return jax.shard_map(
        local,
        mesh=mesh,
        in_specs=placed,
        out_specs=(P(("inner", "outer"), None), P("inner", None), P(("inner", "outer"))),
        check_vma=False,
    )
```

```python
import functools
import math

import jax
import jax.numpy as jnp
from jax import lax
from jax.experimental import pallas as pl
from jax.experimental.pallas import tpu as pltpu
from jax.sharding import PartitionSpec as P


def flipped(block, axis, mask):
    count = lax.axis_size(axis)
    return lax.ppermute(block, axis, [(low, low ^ mask) for low in range(count)])


def exact_dot(a, b, contract):
    return lax.dot_general(
        a, b, (contract, ((), ())), precision=lax.Precision.HIGHEST, preferred_element_type=jnp.float32
    )


def terms(value):
    high = value.astype(jnp.bfloat16).astype(jnp.float32)
    rest = value - high
    middle = rest.astype(jnp.bfloat16).astype(jnp.float32)
    return high, middle, rest - middle


def factor_kernel(block, gram_ref, out_ref, work, lines):
    n = gram_ref.shape[0]
    work[:, :n] = gram_ref[...]
    down = lax.broadcasted_iota(jnp.int32, (n, n), 0)
    across = lax.broadcasted_iota(jnp.int32, (n, n), 1)
    work[:, n:] = jnp.where(down == across, 1.0, 0.0)
    for top in range(0, n, block):
        line = [work[top + i : top + i + 1, :] for i in range(block)]
        corner = {}
        for i in range(block):
            for j in range(i + 1):
                corner[i, j] = jnp.broadcast_to(line[i][:, top + j : top + j + 1], (1, n))
        for j in range(block):
            scale = lax.rsqrt(corner[j, j])
            line[j] = line[j] * jnp.concatenate([scale, scale], axis=1)
            lines[j : j + 1, :] = line[j]
            for i in range(j + 1, block):
                corner[i, j] = corner[i, j] * scale
            for i in range(j + 1, block):
                for m in range(j + 1, i + 1):
                    corner[i, m] = corner[i, m] - corner[i, j] * corner[m, j]
                line[i] = line[i] - jnp.concatenate([corner[i, j]] * 2, axis=1) * line[j]
        done = lines[...]
        out_ref[top : top + block, :] = done[:, n:]
        if top + block < n:
            high, middle, small = terms(done)
            left = jnp.concatenate([high, high, middle, high, small, middle])[:, :n].astype(jnp.bfloat16)
            right = jnp.concatenate([high, middle, high, small, high, middle]).astype(jnp.bfloat16)
            work[...] -= lax.dot_general(
                left, right, (((0,), (0,)), ((), ())), preferred_element_type=jnp.float32
            )


def inverse_factor(gram, block=16):
    n = gram.shape[0]
    return pl.pallas_call(
        functools.partial(factor_kernel, block),
        out_shape=jax.ShapeDtypeStruct((n, n), jnp.float32),
        scratch_shapes=[pltpu.VMEM((n, 2 * n), jnp.float32), pltpu.VMEM((block, 2 * n), jnp.float32)],
        cost_estimate=pl.CostEstimate(flops=6_000_000_000, bytes_accessed=131072, transcendentals=128),
        name="inverse_factor",
    )(gram)


def local(samples, sketch_matrix):
    inner = lax.axis_size("inner")
    outer = lax.axis_size("outer")
    rows, width = samples.shape
    rank = sketch_matrix.shape[1]
    total_rows = rows * inner * outer
    me = lax.axis_index("inner")
    mine = lax.axis_index("outer")
    piece = width // inner
    part = piece // outer
    evens = range(2, inner, 2)

    got = {0: sketch_matrix}
    for mask in reversed(evens):
        got[mask] = flipped(sketch_matrix, "inner", mask)
    even = jnp.concatenate([got[mask] for mask in range(0, inner, 2)])

    def columns(masks):
        return jnp.concatenate(
            [lax.dynamic_slice_in_dim(samples, (me ^ mask) * piece, piece, 1) for mask in masks], axis=1
        )

    even_columns = columns(range(0, inner, 2))
    odd_columns = columns(range(1, inner, 2))
    even, even_columns, odd_columns = lax.optimization_barrier((even, even_columns, odd_columns))
    odd = flipped(even, "inner", 1)
    sketch = jnp.dot(even_columns, even, preferred_element_type=jnp.float32)
    sketch = sketch + jnp.dot(odd_columns, odd, preferred_element_type=jnp.float32)

    gram = exact_dot(sketch, sketch, ((0,), (0,)))
    rounded = lax.reduce_precision(sketch, 8, 7)
    high = rounded.astype(jnp.bfloat16)
    low = (sketch - rounded).astype(jnp.bfloat16)
    both = jnp.concatenate([high, low], axis=1)

    def products(side):
        twice = lax.dot_general(side, both, (((0,), (0,)), ((), ())), preferred_element_type=jnp.float32)
        return twice[:, :rank] + twice[:, rank:]

    gram, both = lax.optimization_barrier((gram, both))
    gram, odd_pieces = lax.optimization_barrier((gram + flipped(gram, "inner", 1), products(odd_columns)))
    pieces = products(even_columns) + flipped(odd_pieces, "inner", 1)
    pieces = pieces.reshape(inner // 2, piece, rank)
    gram = gram + flipped(gram, "outer", 1)
    gram = gram + flipped(gram, "outer", 2)
    own = pieces[0] + flipped(pieces[3], "inner", 6)+ flipped(pieces[1], "inner", 2)+ flipped(pieces[2], "inner", 4)
    gram, own = lax.optimization_barrier((gram, own))
    gram = gram + flipped(gram, "inner", 2)
    gram = gram + flipped(gram, "inner", 4)
    share = lax.dynamic_slice_in_dim(own, mine * part, part, 0)
    for mask in range(1, outer):
        share = share + flipped(
            lax.dynamic_slice_in_dim(own, (mine ^ mask) * part, part, 0), "outer", mask
        )
    gram, share = lax.optimization_barrier((gram, share))

    summed = jnp.zeros((piece, rank), jnp.float32)
    summed = lax.dynamic_update_slice_in_dim(summed, share, mine * part, 0)
    for mask in range(1, outer):
        summed = lax.dynamic_update_slice_in_dim(
            summed, flipped(share, "outer", mask), (mine ^ mask) * part, 0
        )

    inverse = inverse_factor(gram)
    basis = exact_dot(sketch, inverse * math.sqrt(total_rows), ((1,), (1,)))
    basis_low = basis.astype(jnp.bfloat16)
    projection = exact_dot(summed, inverse * (math.sqrt(width) / math.sqrt(total_rows)), ((1,), (1,)))
    projection_low = projection.astype(jnp.bfloat16)

    got = {0: projection_low}
    for mask in reversed(evens):
        got[mask] = flipped(projection_low, "inner", mask)
    even = jnp.concatenate([got[mask] for mask in range(0, inner, 2)])
    odd = flipped(even, "inner", 1)

    def errors(side, factor):
        recon = lax.dot_general(
            basis_low, factor, (((1,), (1,)), ((), ())), preferred_element_type=jnp.float32
        ) * (1.0 / math.sqrt(width))
        diff = side.astype(jnp.float32) - recon
        return jnp.sum(diff * diff, axis=1)

    row_error = (errors(even_columns, even) + errors(odd_columns, odd)) / width
    return (basis, projection, row_error)


def solution(mesh):
    placed = (P(("inner", "outer"), None), P("inner", None))
    return jax.shard_map(
        local,
        mesh=mesh,
        in_specs=placed,
        out_specs=(P(("inner", "outer"), None), P("inner", None), P(("inner", "outer"))),
        check_vma=False,
    )
```

```python
import functools
import math

import jax
import jax.numpy as jnp
from jax import lax
from jax.experimental import pallas as pl
from jax.experimental.pallas import tpu as pltpu
from jax.sharding import PartitionSpec as P


def flipped(block, axis, mask):
    count = lax.axis_size(axis)
    return lax.ppermute(block, axis, [(low, low ^ mask) for low in range(count)])


def exact_dot(a, b, contract):
    return lax.dot_general(
        a, b, (contract, ((), ())), precision=lax.Precision.HIGHEST, preferred_element_type=jnp.float32
    )


def terms(value):
    high = value.astype(jnp.bfloat16).astype(jnp.float32)
    rest = value - high
    middle = rest.astype(jnp.bfloat16).astype(jnp.float32)
    return high, middle, rest - middle


def twice(value):
    return jnp.concatenate([value, value], axis=1)


def eliminate(line, corner, store, side=None, rest=None):
    for j in range(8):
        scale = lax.rsqrt(corner[j, j])
        line[j] = line[j] * twice(scale)
        store(j, line[j][:1])
        for i in range(j + 1, 8):
            corner[i, j] = corner[i, j] * scale
        if side is not None:
            side[j] = side[j] * scale
        for i in range(j + 1, 8):
            for m in range(j + 1, i + 1):
                corner[i, m] = corner[i, m] - corner[i, j] * corner[m, j]
            line[i] = line[i] - twice(corner[i, j]) * line[j]
            if side is not None:
                side[i] = side[i] - corner[i, j] * side[j]
        if side is not None:
            rest = rest - twice(side[j]) * line[j]
    return rest


def factor_kernel(gram_ref, other_ref, out_ref, work, lines):
    n = out_ref.shape[0]
    work[:, :n] = gram_ref[...] + other_ref[...]
    down = lax.broadcasted_iota(jnp.int32, (n, n), 0)
    across = lax.broadcasted_iota(jnp.int32, (n, n), 1)
    work[:, n:] = jnp.where(down == across, 1.0, 0.0)

    def spread(ref, top):
        return [jnp.broadcast_to(ref[top + i : top + i + 1, :], (8, 2 * n)) for i in range(8)]

    def corner_of(line, left):
        return {
            (i, j): jnp.broadcast_to(line[i][:, left + j : left + j + 1], (8, n))
            for i in range(8)
            for j in range(i + 1)
        }

    def store_at(top):
        def store(j, value):
            lines[top + j : top + j + 1, :] = value

        return store

    for top in range(0, n, 16):
        line = spread(work, top)
        below = work[top + 8 : top + 16, :]
        side = [jnp.broadcast_to(below[:, top + j : top + j + 1], (8, n)) for j in range(8)]
        lines[8:, :] = eliminate(line, corner_of(line, top), store_at(0), side, below)
        line = spread(lines, 8)
        eliminate(line, corner_of(line, top + 8), store_at(8))
        done = lines[...]
        out_ref[top : top + 16, :] = done[:, n:]
        if top + 16 < n:
            high, middle, small = terms(done)
            left = jnp.concatenate([high, high, middle, high, small, middle])[:, :n].astype(jnp.bfloat16)
            right = jnp.concatenate([high, middle, high, small, high, middle]).astype(jnp.bfloat16)
            work[...] -= lax.dot_general(
                left, right, (((0,), (0,)), ((), ())), preferred_element_type=jnp.float32
            )


def inverse_factor(*grams):
    n = grams[0].shape[0]
    return pl.pallas_call(
        factor_kernel,
        out_shape=jax.ShapeDtypeStruct((n, n), jnp.float32),
        out_specs=pl.BlockSpec(memory_space=pltpu.VMEM),
        scratch_shapes=[pltpu.VMEM((n, 2 * n), jnp.float32), pltpu.VMEM((16, 2 * n), jnp.float32)],
        cost_estimate=pl.CostEstimate(flops=6_000_000_000, bytes_accessed=131072, transcendentals=128),
        name="inverse_factor",
    )(*grams)


def local(samples, sketch_matrix):
    inner = lax.axis_size("inner")
    outer = lax.axis_size("outer")
    rows, width = samples.shape
    rank = sketch_matrix.shape[1]
    total_rows = rows * inner * outer
    me = lax.axis_index("inner")
    mine = lax.axis_index("outer")
    piece = width // inner
    part = piece // outer
    evens = range(2, inner, 2)

    got = {0: sketch_matrix}
    for mask in reversed(evens):
        got[mask] = flipped(sketch_matrix, "inner", mask)
    even = jnp.concatenate([got[mask] for mask in range(0, inner, 2)])

    def columns(masks):
        return jnp.concatenate(
            [lax.dynamic_slice_in_dim(samples, (me ^ mask) * piece, piece, 1) for mask in masks], axis=1
        )

    even_columns = columns(range(0, inner, 2))
    odd_columns = columns(range(1, inner, 2))
    even, even_columns, odd_columns = lax.optimization_barrier((even, even_columns, odd_columns))
    odd = flipped(even, "inner", 1)
    sketch = jnp.dot(even_columns, even, preferred_element_type=jnp.float32)
    sketch = sketch + jnp.dot(odd_columns, odd, preferred_element_type=jnp.float32)

    gram = exact_dot(sketch, sketch, ((0,), (0,)))
    rounded = lax.reduce_precision(sketch, 8, 7)
    high = rounded.astype(jnp.bfloat16)
    low = (sketch - rounded).astype(jnp.bfloat16)
    both = jnp.concatenate([high, low], axis=1)

    def products(side):
        twice = lax.dot_general(side, both, (((0,), (0,)), ((), ())), preferred_element_type=jnp.float32)
        return twice[:, :rank] + twice[:, rank:]

    gram, both = lax.optimization_barrier((gram, both))
    gram, odd_pieces = lax.optimization_barrier((gram + flipped(gram, "inner", 1), products(odd_columns)))
    pieces = products(even_columns) + flipped(odd_pieces, "inner", 1)
    pieces = pieces.reshape(inner // 2, piece, rank)
    gram = gram + flipped(gram, "outer", 1)
    gram = gram + flipped(gram, "outer", 2)
    own = pieces[0] + flipped(pieces[3], "inner", 6)+ flipped(pieces[1], "inner", 2)+ flipped(pieces[2], "inner", 4)
    gram, own = lax.optimization_barrier((gram, own))
    gram = gram + flipped(gram, "inner", 2)
    last = flipped(gram, "inner", 4)
    share = lax.dynamic_slice_in_dim(own, mine * part, part, 0)
    for mask in range(1, outer):
        share = share + flipped(
            lax.dynamic_slice_in_dim(own, (mine ^ mask) * part, part, 0), "outer", mask
        )
    gram, last, share = lax.optimization_barrier((gram, last, share))

    summed = jnp.zeros((piece, rank), jnp.float32)
    summed = lax.dynamic_update_slice_in_dim(summed, share, mine * part, 0)
    for mask in range(1, outer):
        summed = lax.dynamic_update_slice_in_dim(
            summed, flipped(share, "outer", mask), (mine ^ mask) * part, 0
        )

    inverse = inverse_factor(gram, last)
    basis = exact_dot(sketch, inverse * math.sqrt(total_rows), ((1,), (1,)))
    basis_low = basis.astype(jnp.bfloat16)
    projection = exact_dot(summed, inverse * (math.sqrt(width) / math.sqrt(total_rows)), ((1,), (1,)))
    projection = lax.optimization_barrier(projection)
    projection_low = projection.astype(jnp.bfloat16)

    got = {0: projection_low}
    for mask in reversed(evens):
        got[mask] = flipped(projection_low, "inner", mask)
    even = jnp.concatenate([got[mask] for mask in range(0, inner, 2)])
    odd = flipped(even, "inner", 1)

    def errors(side, factor):
        recon = lax.dot_general(
            basis_low, factor, (((1,), (1,)), ((), ())), preferred_element_type=jnp.float32
        ) * (1.0 / math.sqrt(width))
        diff = side.astype(jnp.float32) - recon
        return jnp.sum(diff * diff, axis=1)

    row_error = (errors(even_columns, even) + errors(odd_columns, odd)) / width
    return (basis, projection, row_error)


def solution(mesh):
    placed = (P(("inner", "outer"), None), P("inner", None))
    return jax.shard_map(
        local,
        mesh=mesh,
        in_specs=placed,
        out_specs=(P(("inner", "outer"), None), P("inner", None), P(("inner", "outer"))),
        check_vma=False,
    )
```

```python
import functools
import math

import jax
import jax.numpy as jnp
from jax import lax
from jax.experimental import pallas as pl
from jax.experimental.pallas import tpu as pltpu
from jax.sharding import PartitionSpec as P


def flipped(block, axis, mask):
    count = lax.axis_size(axis)
    return lax.ppermute(block, axis, [(low, low ^ mask) for low in range(count)])


def exact_dot(a, b, contract):
    return lax.dot_general(
        a, b, (contract, ((), ())), precision=lax.Precision.HIGHEST, preferred_element_type=jnp.float32
    )


def terms(value):
    high = value.astype(jnp.bfloat16).astype(jnp.float32)
    rest = value - high
    middle = rest.astype(jnp.bfloat16).astype(jnp.float32)
    return high, middle, rest - middle


def twice(value):
    return jnp.concatenate([value, value], axis=1)


def eliminate(line, corner, store, side=None, rest=None):
    for j in range(8):
        scale = lax.rsqrt(corner[j, j])
        line[j] = line[j] * twice(scale)
        store(j, line[j][:1])
        for i in range(j + 1, 8):
            corner[i, j] = corner[i, j] * scale
        if side is not None:
            side[j] = side[j] * scale
        for i in range(j + 1, 8):
            for m in range(j + 1, i + 1):
                corner[i, m] = corner[i, m] - corner[i, j] * corner[m, j]
            line[i] = line[i] - twice(corner[i, j]) * line[j]
            if side is not None:
                side[i] = side[i] - corner[i, j] * side[j]
        if side is not None:
            rest = rest - twice(side[j]) * line[j]
    return rest


def factor_kernel(gram_ref, other_ref, out_ref, work, lines):
    n = out_ref.shape[0]
    work[:, :n] = gram_ref[...] + other_ref[...]
    down = lax.broadcasted_iota(jnp.int32, (n, n), 0)
    across = lax.broadcasted_iota(jnp.int32, (n, n), 1)
    work[:, n:] = jnp.where(down == across, 1.0, 0.0)

    def spread(ref, top):
        return [jnp.broadcast_to(ref[top + i : top + i + 1, :], (8, 2 * n)) for i in range(8)]

    def corner_of(line, left):
        return {
            (i, j): jnp.broadcast_to(line[i][:, left + j : left + j + 1], (8, n))
            for i in range(8)
            for j in range(i + 1)
        }

    def store_at(top):
        def store(j, value):
            lines[top + j : top + j + 1, :] = value

        return store

    for top in range(0, n, 16):
        line = spread(work, top)
        below = work[top + 8 : top + 16, :]
        side = [jnp.broadcast_to(below[:, top + j : top + j + 1], (8, n)) for j in range(8)]
        lines[8:, :] = eliminate(line, corner_of(line, top), store_at(0), side, below)
        line = spread(lines, 8)
        eliminate(line, corner_of(line, top + 8), store_at(8))
        done = lines[...]
        out_ref[top : top + 16, :] = done[:, n:]
        if top + 16 < n:
            high, middle, small = terms(done)
            left = jnp.concatenate([high, high, middle, high, small, middle])[:, :n].astype(jnp.bfloat16)
            right = jnp.concatenate([high, middle, high, small, high, middle]).astype(jnp.bfloat16)
            work[...] -= lax.dot_general(
                left, right, (((0,), (0,)), ((), ())), preferred_element_type=jnp.float32
            )


def inverse_factor(*grams):
    n = grams[0].shape[0]
    return pl.pallas_call(
        factor_kernel,
        out_shape=jax.ShapeDtypeStruct((n, n), jnp.float32),
        out_specs=pl.BlockSpec(memory_space=pltpu.VMEM),
        scratch_shapes=[pltpu.VMEM((n, 2 * n), jnp.float32), pltpu.VMEM((16, 2 * n), jnp.float32)],
        cost_estimate=pl.CostEstimate(flops=6_000_000_000, bytes_accessed=131072, transcendentals=128),
        name="inverse_factor",
    )(*grams)


def local(samples, sketch_matrix):
    inner = lax.axis_size("inner")
    outer = lax.axis_size("outer")
    rows, width = samples.shape
    rank = sketch_matrix.shape[1]
    total_rows = rows * inner * outer
    me = lax.axis_index("inner")
    mine = lax.axis_index("outer")
    piece = width // inner
    part = piece // outer
    evens = range(2, inner, 2)

    got = {0: sketch_matrix}
    for mask in reversed(evens):
        got[mask] = flipped(sketch_matrix, "inner", mask)
    even = jnp.concatenate([got[mask] for mask in range(0, inner, 2)])

    def columns(masks):
        return jnp.concatenate(
            [lax.dynamic_slice_in_dim(samples, (me ^ mask) * piece, piece, 1) for mask in masks], axis=1
        )

    even_columns = columns(range(0, inner, 2))
    odd_columns = columns(range(1, inner, 2))
    even, even_columns, odd_columns = lax.optimization_barrier((even, even_columns, odd_columns))
    odd = flipped(even, "inner", 1)
    sketch = jnp.dot(even_columns, even, preferred_element_type=jnp.float32)
    sketch = sketch + jnp.dot(odd_columns, odd, preferred_element_type=jnp.float32)

    gram = exact_dot(sketch, sketch, ((0,), (0,)))
    rounded = lax.reduce_precision(sketch, 8, 7)
    high = rounded.astype(jnp.bfloat16)
    low = (sketch - rounded).astype(jnp.bfloat16)
    both = jnp.concatenate([high, low], axis=1)

    def products(side):
        twice = lax.dot_general(side, both, (((0,), (0,)), ((), ())), preferred_element_type=jnp.float32)
        return twice[:, :rank] + twice[:, rank:]

    gram, both = lax.optimization_barrier((gram, both))
    gram, odd_pieces = lax.optimization_barrier((gram + flipped(gram, "inner", 1), products(odd_columns)))
    pieces = products(even_columns) + flipped(odd_pieces, "inner", 1)
    pieces = pieces.reshape(inner // 2, piece, rank)
    for level in range(outer.bit_length() - 1):
        gram = gram + flipped(gram, "outer", 1 << level)
    own = pieces[0]
    for mask in [inner - 2, *evens[:-1]]:
        own = own + flipped(pieces[mask // 2], "inner", mask)
    gram, own = lax.optimization_barrier((gram, own))
    levels = inner.bit_length() - 1
    for level in range(1, levels - 1):
        gram = gram + flipped(gram, "inner", 1 << level)
    last = flipped(gram, "inner", 1 << (levels - 1))
    share = lax.dynamic_slice_in_dim(own, mine * part, part, 0)
    for mask in range(1, outer):
        share = share + flipped(
            lax.dynamic_slice_in_dim(own, (mine ^ mask) * part, part, 0), "outer", mask
        )
    gram, last, share = lax.optimization_barrier((gram, last, share))

    summed = jnp.zeros((piece, rank), jnp.float32)
    summed = lax.dynamic_update_slice_in_dim(summed, share, mine * part, 0)
    for mask in range(1, outer):
        summed = lax.dynamic_update_slice_in_dim(
            summed, flipped(share, "outer", mask), (mine ^ mask) * part, 0
        )

    inverse = inverse_factor(gram, last)
    basis = exact_dot(sketch, inverse * math.sqrt(total_rows), ((1,), (1,)))
    basis_low = basis.astype(jnp.bfloat16)
    projection = exact_dot(summed, inverse * (math.sqrt(width) / math.sqrt(total_rows)), ((1,), (1,)))
    projection = lax.optimization_barrier(projection)
    projection_low = projection.astype(jnp.bfloat16)

    got = {0: projection_low}
    for mask in reversed(evens):
        got[mask] = flipped(projection_low, "inner", mask)
    even = jnp.concatenate([got[mask] for mask in range(0, inner, 2)])
    odd = flipped(even, "inner", 1)

    def errors(side, factor):
        recon = lax.dot_general(
            basis_low, factor, (((1,), (1,)), ((), ())), preferred_element_type=jnp.float32
        ) * (1.0 / math.sqrt(width))
        diff = side.astype(jnp.float32) - recon
        return jnp.sum(diff * diff, axis=1)

    row_error = (errors(even_columns, even) + errors(odd_columns, odd)) / width
    return (basis, projection, row_error)


def solution(mesh):
    placed = (P(("inner", "outer"), None), P("inner", None))
    return jax.shard_map(
        local,
        mesh=mesh,
        in_specs=placed,
        out_specs=(P(("inner", "outer"), None), P("inner", None), P(("inner", "outer"))),
        check_vma=False,
    )
```

```python
import functools
import math

import jax
import jax.numpy as jnp
from jax import lax
from jax.experimental import pallas as pl
from jax.experimental.pallas import tpu as pltpu
from jax.sharding import PartitionSpec as P


def flipped(block, axis, mask):
    count = lax.axis_size(axis)
    return lax.ppermute(block, axis, [(low, low ^ mask) for low in range(count)])


def exact_dot(a, b, contract):
    return lax.dot_general(
        a, b, (contract, ((), ())), precision=lax.Precision.HIGHEST, preferred_element_type=jnp.float32
    )


def terms(value):
    high = value.astype(jnp.bfloat16).astype(jnp.float32)
    rest = value - high
    middle = rest.astype(jnp.bfloat16).astype(jnp.float32)
    return high, middle, rest - middle


def twice(value):
    return jnp.concatenate([value, value], axis=1)


def eliminate(line, corner, store, side=None, rest=None):
    for j in range(8):
        scale = lax.rsqrt(corner[j, j])
        line[j] = line[j] * twice(scale)
        store(j, line[j][:1])
        for i in range(j + 1, 8):
            corner[i, j] = corner[i, j] * scale
        if side is not None:
            side[j] = side[j] * scale
        for i in range(j + 1, 8):
            for m in range(j + 1, i + 1):
                corner[i, m] = corner[i, m] - corner[i, j] * corner[m, j]
            line[i] = line[i] - twice(corner[i, j]) * line[j]
            if side is not None:
                side[i] = side[i] - corner[i, j] * side[j]
        if side is not None:
            rest = rest - twice(side[j]) * line[j]
    return rest


def factor_kernel(gram_ref, other_ref, out_ref, work, lines):
    n = out_ref.shape[0]
    work[:, :n] = gram_ref[...] + other_ref[...]
    down = lax.broadcasted_iota(jnp.int32, (n, n), 0)
    across = lax.broadcasted_iota(jnp.int32, (n, n), 1)
    work[:, n:] = jnp.where(down == across, 1.0, 0.0)

    def spread(ref, top):
        return [jnp.broadcast_to(ref[top + i : top + i + 1, :], (8, 2 * n)) for i in range(8)]

    def corner_of(line, left):
        return {
            (i, j): jnp.broadcast_to(line[i][:, left + j : left + j + 1], (8, n))
            for i in range(8)
            for j in range(i + 1)
        }

    def store_at(top):
        def store(j, value):
            lines[top + j : top + j + 1, :] = value

        return store

    for top in range(0, n, 16):
        line = spread(work, top)
        below = work[top + 8 : top + 16, :]
        side = [jnp.broadcast_to(below[:, top + j : top + j + 1], (8, n)) for j in range(8)]
        lines[8:, :] = eliminate(line, corner_of(line, top), store_at(0), side, below)
        line = spread(lines, 8)
        eliminate(line, corner_of(line, top + 8), store_at(8))
        done = lines[...]
        out_ref[top : top + 16, :] = done[:, n:]
        if top + 16 < n:
            high, middle, small = terms(done)
            left = jnp.concatenate([high, high, middle, high, small, middle])[:, :n].astype(jnp.bfloat16)
            right = jnp.concatenate([high, middle, high, small, high, middle]).astype(jnp.bfloat16)
            work[...] -= lax.dot_general(
                left, right, (((0,), (0,)), ((), ())), preferred_element_type=jnp.float32
            )


def inverse_factor(*grams):
    n = grams[0].shape[0]
    return pl.pallas_call(
        factor_kernel,
        out_shape=jax.ShapeDtypeStruct((n, n), jnp.float32),
        out_specs=pl.BlockSpec(memory_space=pltpu.VMEM),
        scratch_shapes=[pltpu.VMEM((n, 2 * n), jnp.float32), pltpu.VMEM((16, 2 * n), jnp.float32)],
        cost_estimate=pl.CostEstimate(flops=6_000_000_000, bytes_accessed=131072, transcendentals=128),
        compiler_params=pltpu.CompilerParams(vmem_limit_bytes=4 * 1024 * 1024),
        name="inverse_factor",
    )(*grams)


def local(samples, sketch_matrix):
    inner = lax.axis_size("inner")
    outer = lax.axis_size("outer")
    rows, width = samples.shape
    rank = sketch_matrix.shape[1]
    total_rows = rows * inner * outer
    me = lax.axis_index("inner")
    mine = lax.axis_index("outer")
    piece = width // inner
    part = piece // outer
    evens = range(2, inner, 2)

    got = {0: sketch_matrix}
    for mask in reversed(evens):
        got[mask] = flipped(sketch_matrix, "inner", mask)
    even = jnp.concatenate([got[mask] for mask in range(0, inner, 2)])

    def columns(masks):
        return jnp.concatenate(
            [lax.dynamic_slice_in_dim(samples, (me ^ mask) * piece, piece, 1) for mask in masks], axis=1
        )

    even_columns = columns(range(0, inner, 2))
    odd_columns = columns(range(1, inner, 2))
    even, even_columns, odd_columns = lax.optimization_barrier((even, even_columns, odd_columns))
    odd = flipped(even, "inner", 1)
    sketch = jnp.dot(even_columns, even, preferred_element_type=jnp.float32)
    sketch = sketch + jnp.dot(odd_columns, odd, preferred_element_type=jnp.float32)

    gram = exact_dot(sketch, sketch, ((0,), (0,)))
    rounded = lax.reduce_precision(sketch, 8, 7)
    high = rounded.astype(jnp.bfloat16)
    low = (sketch - rounded).astype(jnp.bfloat16)
    both = jnp.concatenate([high, low], axis=1)

    def products(side):
        twice = lax.dot_general(side, both, (((0,), (0,)), ((), ())), preferred_element_type=jnp.float32)
        return twice[:, :rank] + twice[:, rank:]

    gram, both = lax.optimization_barrier((gram, both))
    gram, odd_pieces = lax.optimization_barrier((gram + flipped(gram, "inner", 1), products(odd_columns)))
    pieces = products(even_columns) + flipped(odd_pieces, "inner", 1)
    pieces = pieces.reshape(inner // 2, piece, rank)
    for level in range(outer.bit_length() - 1):
        gram = gram + flipped(gram, "outer", 1 << level)
    own = pieces[0]
    for mask in [inner - 2, *evens[:-1]]:
        own = own + flipped(pieces[mask // 2], "inner", mask)
    gram, own = lax.optimization_barrier((gram, own))
    levels = inner.bit_length() - 1
    for level in range(1, levels - 1):
        gram = gram + flipped(gram, "inner", 1 << level)
    last = flipped(gram, "inner", 1 << (levels - 1))
    share = lax.dynamic_slice_in_dim(own, mine * part, part, 0)
    for mask in range(1, outer):
        share = share + flipped(
            lax.dynamic_slice_in_dim(own, (mine ^ mask) * part, part, 0), "outer", mask
        )
    gram, last, share = lax.optimization_barrier((gram, last, share))

    summed = jnp.zeros((piece, rank), jnp.float32)
    summed = lax.dynamic_update_slice_in_dim(summed, share, mine * part, 0)
    for mask in range(1, outer):
        summed = lax.dynamic_update_slice_in_dim(
            summed, flipped(share, "outer", mask), (mine ^ mask) * part, 0
        )

    inverse = inverse_factor(gram, last)
    basis = exact_dot(sketch, inverse * math.sqrt(total_rows), ((1,), (1,)))
    basis_low = basis.astype(jnp.bfloat16)
    projection = exact_dot(summed, inverse * (math.sqrt(width) / math.sqrt(total_rows)), ((1,), (1,)))
    projection = lax.optimization_barrier(projection)
    projection_low = projection.astype(jnp.bfloat16)

    got = {0: projection_low}
    for mask in reversed(evens):
        got[mask] = flipped(projection_low, "inner", mask)
    even = jnp.concatenate([got[mask] for mask in range(0, inner, 2)])
    odd = flipped(even, "inner", 1)

    def errors(side, factor):
        recon = lax.dot_general(
            basis_low, factor, (((1,), (1,)), ((), ())), preferred_element_type=jnp.float32
        ) * (1.0 / math.sqrt(width))
        diff = side.astype(jnp.float32) - recon
        return jnp.sum(diff * diff, axis=1)

    row_error = (errors(even_columns, even) + errors(odd_columns, odd)) / width
    return (basis, projection, row_error)


def solution(mesh):
    placed = (P(("inner", "outer"), None), P("inner", None))
    return jax.shard_map(
        local,
        mesh=mesh,
        in_specs=placed,
        out_specs=(P(("inner", "outer"), None), P("inner", None), P(("inner", "outer"))),
        check_vma=False,
    )
```

```python
import functools
import math

import jax
import jax.numpy as jnp
from jax import lax
from jax.experimental import pallas as pl
from jax.experimental.pallas import tpu as pltpu
from jax.sharding import PartitionSpec as P


def flipped(block, axis, mask):
    count = lax.axis_size(axis)
    return lax.ppermute(block, axis, [(low, low ^ mask) for low in range(count)])


def exact_dot(a, b, contract):
    return lax.dot_general(
        a, b, (contract, ((), ())), precision=lax.Precision.HIGHEST, preferred_element_type=jnp.float32
    )


def terms(value):
    high = value.astype(jnp.bfloat16).astype(jnp.float32)
    rest = value - high
    middle = rest.astype(jnp.bfloat16).astype(jnp.float32)
    return high, middle, rest - middle


def twice(value):
    return jnp.concatenate([value, value], axis=1)


def eliminate(line, corner, store, side=None, rest=None):
    for j in range(8):
        scale = lax.rsqrt(corner[j, j])
        line[j] = line[j] * twice(scale)
        store(j, line[j][:1])
        for i in range(j + 1, 8):
            corner[i, j] = corner[i, j] * scale
        if side is not None:
            side[j] = side[j] * scale
        for i in range(j + 1, 8):
            for m in range(j + 1, i + 1):
                corner[i, m] = corner[i, m] - corner[i, j] * corner[m, j]
            line[i] = line[i] - twice(corner[i, j]) * line[j]
            if side is not None:
                side[i] = side[i] - corner[i, j] * side[j]
        if side is not None:
            rest = rest - twice(side[j]) * line[j]
    return rest


def factor_kernel(gram_ref, other_ref, out_ref, work, lines):
    n = out_ref.shape[0]
    work[:, :n] = gram_ref[...] + other_ref[...]
    down = lax.broadcasted_iota(jnp.int32, (n, n), 0)
    across = lax.broadcasted_iota(jnp.int32, (n, n), 1)
    work[:, n:] = jnp.where(down == across, 1.0, 0.0)

    def spread(ref, top):
        return [jnp.broadcast_to(ref[top + i : top + i + 1, :], (8, 2 * n)) for i in range(8)]

    def corner_of(line, left):
        return {
            (i, j): jnp.broadcast_to(line[i][:, left + j : left + j + 1], (8, n))
            for i in range(8)
            for j in range(i + 1)
        }

    def store_at(top):
        def store(j, value):
            lines[top + j : top + j + 1, :] = value

        return store

    for top in range(0, n, 16):
        line = spread(work, top)
        below = work[top + 8 : top + 16, :]
        side = [jnp.broadcast_to(below[:, top + j : top + j + 1], (8, n)) for j in range(8)]
        lines[8:, :] = eliminate(line, corner_of(line, top), store_at(0), side, below)
        line = spread(lines, 8)
        eliminate(line, corner_of(line, top + 8), store_at(8))
        done = lines[...]
        out_ref[top : top + 16, :] = done[:, n:]
        if top + 16 < n:
            high, middle, small = terms(done)
            left = jnp.concatenate([high, high, middle, high, small, middle])[:, :n].astype(jnp.bfloat16)
            right = jnp.concatenate([high, middle, high, small, high, middle]).astype(jnp.bfloat16)
            work[...] -= lax.dot_general(
                left, right, (((0,), (0,)), ((), ())), preferred_element_type=jnp.float32
            )


def inverse_factor(*grams):
    n = grams[0].shape[0]
    return pl.pallas_call(
        factor_kernel,
        out_shape=jax.ShapeDtypeStruct((n, n), jnp.float32),
        out_specs=pl.BlockSpec(memory_space=pltpu.VMEM),
        scratch_shapes=[pltpu.VMEM((n, 2 * n), jnp.float32), pltpu.VMEM((16, 2 * n), jnp.float32)],
        cost_estimate=pl.CostEstimate(flops=6_000_000_000, bytes_accessed=131072, transcendentals=128),
        compiler_params=pltpu.CompilerParams(vmem_limit_bytes=4 * 1024 * 1024),
        name="inverse_factor",
    )(*grams)


def local(samples, sketch_matrix):
    inner = lax.axis_size("inner")
    outer = lax.axis_size("outer")
    rows, width = samples.shape
    rank = sketch_matrix.shape[1]
    total_rows = rows * inner * outer
    me = lax.axis_index("inner")
    mine = lax.axis_index("outer")
    piece = width // inner
    part = piece // outer
    evens = range(2, inner, 2)

    got = {0: sketch_matrix}
    for mask in reversed(evens):
        got[mask] = flipped(sketch_matrix, "inner", mask)
    even = jnp.concatenate([got[mask] for mask in range(0, inner, 2)])

    def columns(masks):
        return jnp.concatenate(
            [lax.dynamic_slice_in_dim(samples, (me ^ mask) * piece, piece, 1) for mask in masks], axis=1
        )

    even_columns = columns(range(0, inner, 2))
    odd_columns = columns(range(1, inner, 2))
    even, even_columns, odd_columns = lax.optimization_barrier((even, even_columns, odd_columns))
    odd = flipped(even, "inner", 1)
    sketch = jnp.dot(even_columns, even, preferred_element_type=jnp.float32)
    sketch = sketch + jnp.dot(odd_columns, odd, preferred_element_type=jnp.float32)

    gram = exact_dot(sketch, sketch, ((0,), (0,)))
    rounded = lax.reduce_precision(sketch, 8, 7)
    high = rounded.astype(jnp.bfloat16)
    low = (sketch - rounded).astype(jnp.bfloat16)
    both = jnp.concatenate([high, low], axis=1)

    def products(side):
        twice = lax.dot_general(side, both, (((0,), (0,)), ((), ())), preferred_element_type=jnp.float32)
        return twice[:, :rank] + twice[:, rank:]

    gram = gram + flipped(gram, "inner", 1)
    pieces = products(even_columns) + flipped(products(odd_columns), "inner", 1)
    pieces = pieces.reshape(inner // 2, piece, rank)
    for level in range(outer.bit_length() - 1):
        gram = gram + flipped(gram, "outer", 1 << level)
    own = pieces[0]
    for mask in [inner - 2, *evens[:-1]]:
        own = own + flipped(pieces[mask // 2], "inner", mask)
    gram, own = lax.optimization_barrier((gram, own))
    levels = inner.bit_length() - 1
    for level in range(1, levels - 1):
        gram = gram + flipped(gram, "inner", 1 << level)
    last = flipped(gram, "inner", 1 << (levels - 1))
    parts = [lax.dynamic_slice_in_dim(own, (mine ^ mask) * part, part, 0) for mask in range(outer)]
    parts = lax.optimization_barrier(parts)
    share = parts[0]
    for mask in range(1, outer):
        share = share + flipped(parts[mask], "outer", mask)
    gram, last, share = lax.optimization_barrier((gram, last, share))

    summed = jnp.zeros((piece, rank), jnp.float32)
    summed = lax.dynamic_update_slice_in_dim(summed, share, mine * part, 0)
    for mask in reversed(range(1, outer)):
        summed = lax.dynamic_update_slice_in_dim(
            summed, flipped(share, "outer", mask), (mine ^ mask) * part, 0
        )

    inverse = inverse_factor(gram, last)
    basis = exact_dot(sketch, inverse * math.sqrt(total_rows), ((1,), (1,)))
    basis_low = basis.astype(jnp.bfloat16)
    projection = exact_dot(summed, inverse * (math.sqrt(width) / math.sqrt(total_rows)), ((1,), (1,)))
    projection = lax.optimization_barrier(projection)
    projection_low = projection.astype(jnp.bfloat16)

    got = {0: projection_low}
    for mask in reversed(evens):
        got[mask] = flipped(projection_low, "inner", mask)
    even = jnp.concatenate([got[mask] for mask in range(0, inner, 2)])
    odd = flipped(even, "inner", 1)

    def errors(side, factor):
        recon = lax.dot_general(
            basis_low, factor, (((1,), (1,)), ((), ())), preferred_element_type=jnp.float32
        ) * (1.0 / math.sqrt(width))
        diff = side.astype(jnp.float32) - recon
        return jnp.sum(diff * diff, axis=1)

    row_error = (errors(even_columns, even) + errors(odd_columns, odd)) / width
    return (basis, projection, row_error)


def solution(mesh):
    placed = (P(("inner", "outer"), None), P("inner", None))
    return jax.shard_map(
        local,
        mesh=mesh,
        in_specs=placed,
        out_specs=(P(("inner", "outer"), None), P("inner", None), P(("inner", "outer"))),
        check_vma=False,
    )
```

```python
import functools
import math

import jax
import jax.numpy as jnp
from jax import lax
from jax.experimental import pallas as pl
from jax.experimental.pallas import tpu as pltpu
from jax.sharding import PartitionSpec as P


def flipped(block, axis, mask):
    count = lax.axis_size(axis)
    return lax.ppermute(block, axis, [(low, low ^ mask) for low in range(count)])


def exact_dot(a, b, contract):
    return lax.dot_general(
        a, b, (contract, ((), ())), precision=lax.Precision.HIGHEST, preferred_element_type=jnp.float32
    )


def terms(value):
    high = value.astype(jnp.bfloat16).astype(jnp.float32)
    rest = value - high
    middle = rest.astype(jnp.bfloat16).astype(jnp.float32)
    return high, middle, rest - middle


def twice(value):
    return jnp.concatenate([value, value], axis=1)


def eliminate(line, corner, store, side=None, rest=None):
    for j in range(8):
        scale = lax.rsqrt(corner[j, j])
        line[j] = line[j] * twice(scale)
        store(j, line[j][:1])
        for i in range(j + 1, 8):
            corner[i, j] = corner[i, j] * scale
        if side is not None:
            side[j] = side[j] * scale
        for i in range(j + 1, 8):
            for m in range(j + 1, i + 1):
                corner[i, m] = corner[i, m] - corner[i, j] * corner[m, j]
            line[i] = line[i] - twice(corner[i, j]) * line[j]
            if side is not None:
                side[i] = side[i] - corner[i, j] * side[j]
        if side is not None:
            rest = rest - twice(side[j]) * line[j]
    return rest


def factor_kernel(gram_ref, other_ref, out_ref, work, lines):
    n = out_ref.shape[0]
    work[:, :n] = gram_ref[...] + other_ref[...]
    down = lax.broadcasted_iota(jnp.int32, (n, n), 0)
    across = lax.broadcasted_iota(jnp.int32, (n, n), 1)
    work[:, n:] = jnp.where(down == across, 1.0, 0.0)

    def spread(ref, top):
        return [jnp.broadcast_to(ref[top + i : top + i + 1, :], (8, 2 * n)) for i in range(8)]

    def corner_of(line, left):
        return {
            (i, j): jnp.broadcast_to(line[i][:, left + j : left + j + 1], (8, n))
            for i in range(8)
            for j in range(i + 1)
        }

    def store_at(top):
        def store(j, value):
            lines[top + j : top + j + 1, :] = value

        return store

    for top in range(0, n, 16):
        line = spread(work, top)
        below = work[top + 8 : top + 16, :]
        side = [jnp.broadcast_to(below[:, top + j : top + j + 1], (8, n)) for j in range(8)]
        lines[8:, :] = eliminate(line, corner_of(line, top), store_at(0), side, below)
        line = spread(lines, 8)
        eliminate(line, corner_of(line, top + 8), store_at(8))
        done = lines[...]
        out_ref[top : top + 16, :] = done[:, n:]
        if top + 16 < n:
            high, middle, small = terms(done)
            left = jnp.concatenate([high, high, middle, high, small, middle])[:, :n].astype(jnp.bfloat16)
            right = jnp.concatenate([high, middle, high, small, high, middle]).astype(jnp.bfloat16)
            work[...] -= lax.dot_general(
                left, right, (((0,), (0,)), ((), ())), preferred_element_type=jnp.float32
            )


def inverse_factor(*grams):
    n = grams[0].shape[0]
    return pl.pallas_call(
        factor_kernel,
        out_shape=jax.ShapeDtypeStruct((n, n), jnp.float32),
        out_specs=pl.BlockSpec(memory_space=pltpu.VMEM),
        scratch_shapes=[pltpu.VMEM((n, 2 * n), jnp.float32), pltpu.VMEM((16, 2 * n), jnp.float32)],
        cost_estimate=pl.CostEstimate(flops=6_000_000_000, bytes_accessed=131072, transcendentals=128),
        compiler_params=pltpu.CompilerParams(vmem_limit_bytes=4 * 1024 * 1024),
        name="inverse_factor",
    )(*grams)


def local(samples, sketch_matrix):
    inner = lax.axis_size("inner")
    outer = lax.axis_size("outer")
    rows, width = samples.shape
    rank = sketch_matrix.shape[1]
    total_rows = rows * inner * outer
    me = lax.axis_index("inner")
    mine = lax.axis_index("outer")
    piece = width // inner
    part = piece // outer
    evens = range(2, inner, 2)

    got = {0: sketch_matrix}
    for mask in reversed(evens):
        got[mask] = flipped(sketch_matrix, "inner", mask)
    even = jnp.concatenate([got[mask] for mask in range(0, inner, 2)])

    def columns(masks):
        return jnp.concatenate(
            [lax.dynamic_slice_in_dim(samples, (me ^ mask) * piece, piece, 1) for mask in masks], axis=1
        )

    even_columns = columns(range(0, inner, 2))
    odd_columns = columns(range(1, inner, 2))
    even, even_columns, odd_columns = lax.optimization_barrier((even, even_columns, odd_columns))
    odd = flipped(even, "inner", 1)
    sketch = jnp.dot(even_columns, even, preferred_element_type=jnp.float32)
    sketch = sketch + jnp.dot(odd_columns, odd, preferred_element_type=jnp.float32)

    gram = exact_dot(sketch, sketch, ((0,), (0,)))
    rounded = lax.reduce_precision(sketch, 8, 7)
    high = rounded.astype(jnp.bfloat16)
    low = (sketch - rounded).astype(jnp.bfloat16)
    both = jnp.concatenate([high, low], axis=1)

    def products(side):
        twice = lax.dot_general(side, both, (((0,), (0,)), ((), ())), preferred_element_type=jnp.float32)
        return twice[:, :rank] + twice[:, rank:]

    gram = gram + flipped(gram, "inner", 1)
    pieces = products(even_columns) + flipped(products(odd_columns), "inner", 1)
    pieces = pieces.reshape(inner // 2, piece, rank)
    for level in range(outer.bit_length() - 1):
        gram = gram + flipped(gram, "outer", 1 << level)
    own = pieces[0]
    for mask in [inner - 2, *evens[:-1]]:
        own = own + flipped(pieces[mask // 2], "inner", mask)
    gram, own = lax.optimization_barrier((gram, own))
    levels = inner.bit_length() - 1
    for level in range(1, levels - 1):
        gram = gram + flipped(gram, "inner", 1 << level)
    last = flipped(gram, "inner", 1 << (levels - 1))
    parts = [lax.dynamic_slice_in_dim(own, (mine ^ mask) * part, part, 0) for mask in range(outer)]
    parts = lax.optimization_barrier(parts)
    share = parts[0]
    for mask in range(1, outer):
        share = share + flipped(parts[mask], "outer", mask)

    summed = jnp.zeros((piece, rank), jnp.float32)
    summed = lax.dynamic_update_slice_in_dim(summed, share, mine * part, 0)
    for mask in reversed(range(1, outer)):
        summed = lax.dynamic_update_slice_in_dim(
            summed, flipped(share, "outer", mask), (mine ^ mask) * part, 0
        )

    inverse = inverse_factor(gram, last)
    basis = exact_dot(sketch, inverse * math.sqrt(total_rows), ((1,), (1,)))
    basis_low = basis.astype(jnp.bfloat16)
    projection = exact_dot(summed, inverse * (math.sqrt(width) / math.sqrt(total_rows)), ((1,), (1,)))
    projection = lax.optimization_barrier(projection)
    projection_low = projection.astype(jnp.bfloat16)

    got = {0: projection_low}
    for mask in reversed(evens):
        got[mask] = flipped(projection_low, "inner", mask)
    even = jnp.concatenate([got[mask] for mask in range(0, inner, 2)])
    odd = flipped(even, "inner", 1)

    def errors(side, factor):
        recon = lax.dot_general(
            basis_low, factor, (((1,), (1,)), ((), ())), preferred_element_type=jnp.float32
        ) * (1.0 / math.sqrt(width))
        diff = side.astype(jnp.float32) - recon
        return jnp.sum(diff * diff, axis=1)

    row_error = (errors(even_columns, even) + errors(odd_columns, odd)) / width
    return (basis, projection, row_error)


def solution(mesh):
    placed = (P(("inner", "outer"), None), P("inner", None))
    return jax.shard_map(
        local,
        mesh=mesh,
        in_specs=placed,
        out_specs=(P(("inner", "outer"), None), P("inner", None), P(("inner", "outer"))),
        check_vma=False,
    )
```

```python
import functools
import math

import jax
import jax.numpy as jnp
from jax import lax
from jax.experimental import pallas as pl
from jax.experimental.pallas import tpu as pltpu
from jax.sharding import PartitionSpec as P


def flipped(block, axis, mask):
    count = lax.axis_size(axis)
    return lax.ppermute(block, axis, [(low, low ^ mask) for low in range(count)])


def exact_dot(a, b, contract):
    return lax.dot_general(
        a, b, (contract, ((), ())), precision=lax.Precision.HIGHEST, preferred_element_type=jnp.float32
    )


def terms(value):
    high = value.astype(jnp.bfloat16).astype(jnp.float32)
    rest = value - high
    middle = rest.astype(jnp.bfloat16).astype(jnp.float32)
    return high, middle, rest - middle


def twice(value):
    return jnp.concatenate([value, value], axis=1)


def eliminate(line, corner, store, side=None, rest=None):
    for j in range(8):
        scale = lax.rsqrt(corner[j, j])
        line[j] = line[j] * twice(scale)
        store(j, line[j][:1])
        for i in range(j + 1, 8):
            corner[i, j] = corner[i, j] * scale
        if side is not None:
            side[j] = side[j] * scale
        for i in range(j + 1, 8):
            for m in range(j + 1, i + 1):
                corner[i, m] = corner[i, m] - corner[i, j] * corner[m, j]
            line[i] = line[i] - twice(corner[i, j]) * line[j]
            if side is not None:
                side[i] = side[i] - corner[i, j] * side[j]
        if side is not None:
            rest = rest - twice(side[j]) * line[j]
    return rest


def factor_kernel(gram_ref, other_ref, out_ref, work, lines):
    n = out_ref.shape[0]
    work[:, :n] = gram_ref[...] + other_ref[...]
    down = lax.broadcasted_iota(jnp.int32, (n, n), 0)
    across = lax.broadcasted_iota(jnp.int32, (n, n), 1)
    work[:, n:] = jnp.where(down == across, 1.0, 0.0)

    def spread(ref, top):
        return [jnp.broadcast_to(ref[top + i : top + i + 1, :], (8, 2 * n)) for i in range(8)]

    def corner_of(line, left):
        return {
            (i, j): jnp.broadcast_to(line[i][:, left + j : left + j + 1], (8, n))
            for i in range(8)
            for j in range(i + 1)
        }

    def store_at(top):
        def store(j, value):
            lines[top + j : top + j + 1, :] = value

        return store

    for top in range(0, n, 16):
        line = spread(work, top)
        below = work[top + 8 : top + 16, :]
        side = [jnp.broadcast_to(below[:, top + j : top + j + 1], (8, n)) for j in range(8)]
        lines[8:, :] = eliminate(line, corner_of(line, top), store_at(0), side, below)
        line = spread(lines, 8)
        eliminate(line, corner_of(line, top + 8), store_at(8))
        done = lines[...]
        out_ref[top : top + 16, :] = done[:, n:]
        if top + 16 < n:
            high, middle, small = terms(done)
            left = jnp.concatenate([high, high, middle, high, small, middle])[:, :n].astype(jnp.bfloat16)
            right = jnp.concatenate([high, middle, high, small, high, middle]).astype(jnp.bfloat16)
            work[...] -= lax.dot_general(
                left, right, (((0,), (0,)), ((), ())), preferred_element_type=jnp.float32
            )


def inverse_factor(*grams):
    n = grams[0].shape[0]
    return pl.pallas_call(
        factor_kernel,
        out_shape=jax.ShapeDtypeStruct((n, n), jnp.float32),
        out_specs=pl.BlockSpec(memory_space=pltpu.VMEM),
        scratch_shapes=[pltpu.VMEM((n, 2 * n), jnp.float32), pltpu.VMEM((16, 2 * n), jnp.float32)],
        cost_estimate=pl.CostEstimate(flops=6_000_000_000, bytes_accessed=131072, transcendentals=128),
        compiler_params=pltpu.CompilerParams(vmem_limit_bytes=4 * 1024 * 1024),
        name="inverse_factor",
    )(*grams)


def local(samples, sketch_matrix):
    inner = lax.axis_size("inner")
    outer = lax.axis_size("outer")
    rows, width = samples.shape
    rank = sketch_matrix.shape[1]
    total_rows = rows * inner * outer
    me = lax.axis_index("inner")
    mine = lax.axis_index("outer")
    piece = width // inner
    part = piece // outer
    evens = range(2, inner, 2)

    got = {0: sketch_matrix}
    for mask in reversed(evens):
        got[mask] = flipped(sketch_matrix, "inner", mask)
    even = jnp.concatenate([got[mask] for mask in range(0, inner, 2)])

    def columns(masks):
        return jnp.concatenate(
            [lax.dynamic_slice_in_dim(samples, (me ^ mask) * piece, piece, 1) for mask in masks], axis=1
        )

    even_columns = columns(range(0, inner, 2))
    odd_columns = columns(range(1, inner, 2))
    even, even_columns, odd_columns = lax.optimization_barrier((even, even_columns, odd_columns))
    odd = flipped(even, "inner", 1)
    sketch = jnp.dot(even_columns, even, preferred_element_type=jnp.float32)
    sketch = sketch + jnp.dot(odd_columns, odd, preferred_element_type=jnp.float32)

    gram = exact_dot(sketch, sketch, ((0,), (0,)))
    rounded = lax.reduce_precision(sketch, 8, 7)
    high = rounded.astype(jnp.bfloat16)
    low = (sketch - rounded).astype(jnp.bfloat16)
    both = jnp.concatenate([high, low], axis=1)

    def products(side):
        twice = lax.dot_general(side, both, (((0,), (0,)), ((), ())), preferred_element_type=jnp.float32)
        return twice[:, :rank] + twice[:, rank:]

    gram = gram + flipped(gram, "inner", 1)
    pieces = products(even_columns) + flipped(products(odd_columns), "inner", 1)
    pieces = pieces.reshape(inner // 2, piece, rank)
    for level in range(outer.bit_length() - 1):
        gram = gram + flipped(gram, "outer", 1 << level)
    own = pieces[0]
    for mask in [inner - 2, *evens[:-1]]:
        own = own + flipped(pieces[mask // 2], "inner", mask)
    levels = inner.bit_length() - 1
    for level in range(1, levels - 1):
        gram = gram + flipped(gram, "inner", 1 << level)
    last = flipped(gram, "inner", 1 << (levels - 1))
    parts = [lax.dynamic_slice_in_dim(own, (mine ^ mask) * part, part, 0) for mask in range(outer)]
    parts = lax.optimization_barrier(parts)
    share = parts[0]
    for mask in range(1, outer):
        share = share + flipped(parts[mask], "outer", mask)

    summed = jnp.zeros((piece, rank), jnp.float32)
    summed = lax.dynamic_update_slice_in_dim(summed, share, mine * part, 0)
    for mask in reversed(range(1, outer)):
        summed = lax.dynamic_update_slice_in_dim(
            summed, flipped(share, "outer", mask), (mine ^ mask) * part, 0
        )

    inverse = inverse_factor(gram, last)
    basis = exact_dot(sketch, inverse * math.sqrt(total_rows), ((1,), (1,)))
    basis_low = basis.astype(jnp.bfloat16)
    projection = exact_dot(summed, inverse * (math.sqrt(width) / math.sqrt(total_rows)), ((1,), (1,)))
    projection = lax.optimization_barrier(projection)
    projection_low = projection.astype(jnp.bfloat16)

    got = {0: projection_low}
    for mask in reversed(evens):
        got[mask] = flipped(projection_low, "inner", mask)
    even = jnp.concatenate([got[mask] for mask in range(0, inner, 2)])
    odd = flipped(even, "inner", 1)

    def errors(side, factor):
        recon = lax.dot_general(
            basis_low, factor, (((1,), (1,)), ((), ())), preferred_element_type=jnp.float32
        ) * (1.0 / math.sqrt(width))
        diff = side.astype(jnp.float32) - recon
        return jnp.sum(diff * diff, axis=1)

    row_error = (errors(even_columns, even) + errors(odd_columns, odd)) / width
    return (basis, projection, row_error)


def solution(mesh):
    placed = (P(("inner", "outer"), None), P("inner", None))
    return jax.shard_map(
        local,
        mesh=mesh,
        in_specs=placed,
        out_specs=(P(("inner", "outer"), None), P("inner", None), P(("inner", "outer"))),
        check_vma=False,
    )
```
